32 devices in a mesh: tm: 4 (over z), sta: 8 (over y, x, core).
Axes of the slice: x: 2, y: 2, z: 4, core: 2. Of those that a mesh axis runs over, the one named last changes fastest.
Arguments:
- record: bfloat16 [128, 2048], P('sta', 'tm')
- tail: bfloat16 [128, 454], P('sta')
- templates: bfloat16 [128, 200, 512], P('sta'), may hold values from -6 to 6
- live: int32 [128], P('sta'), may hold values 0 or 1
- det_template: int32 [56], P('tm'), may hold values from 0 to 511
- det_start: int32 [56], P('tm'), may hold values from 0 to 2047, as said below
- det_owner: int32 [56], P('tm'), may hold values from 0 to 7, as said below
- det_mask: int32 [56, 128], P('tm', 'sta'), may hold values 0 or 1
Outputs:
- stack: float32 [512, 2048], P('sta', 'tm')
- xcorr: bfloat16 [128, 128, 256], P(('tm', 'sta'))
The draws below stay inside these ranges and needn't reach their ends.
Inputs may be any that keep to these rules, and one draw needn't show every extreme that they name: `det_start`: the detections of rows b * 14 to (b + 1) * 14 - 1 have their cutouts starting within time block b, samples b * 512 to (b + 1) * 512 - 1. `det_owner`: within the 14 rows of one time block no owner appears more than 4 times, and some owner appears exactly 4 times.
All inputs are finite; a program needn't handle non-finite values. No bound on the sum of `live` or of `det_mask` on one device may be relied on, other than what follows from the above.
Results may differ from the reference program's by a relative error of at most 0.0057.
Values may be sent and summed in bfloat16 or wider, within the bound.
A program may use at most 128 MiB of HBM per device.

```python
import math
import jax
import jax.numpy as jnp
from jax import lax

K = 512
L = 200
NLAG = 256
CAP = 4
TS = 512
CUT = 455
TIME = 2048
CHANNELS = 128
DET_BLK = 14
DETS = 56
SLOTS = 128
N_TM = 4
N_STA = 8


def channel_gain(key):
    return jnp.exp(jax.random.uniform(jax.random.fold_in(key, 11), (CHANNELS, 1), jnp.float32, 0.0, math.log(10.0)))


def baseline_drift(key):
    spacing = max(L // 4, 1)
    total_len = TIME + CUT - 1
    knot_count = total_len // spacing + 2
    polarity_key, baseline_key, wander_key = jax.random.split(jax.random.fold_in(key, 13), 3)
    polarity = (2 * jax.random.randint(polarity_key, (CHANNELS, 1), 0, 2, jnp.int32) - 1).astype(jnp.float32)
    baseline = polarity * jax.random.uniform(baseline_key, (CHANNELS, 1), jnp.float32, 2.0, 5.0)
    knots = baseline + 1.5 * jax.random.normal(wander_key, (CHANNELS, knot_count), jnp.float32)
    position = jnp.arange(total_len, dtype=jnp.int32)
    knot_index = (position // spacing).astype(jnp.int32)
    fraction = (position % spacing).astype(jnp.float32) / spacing
    return jnp.take(knots, knot_index, axis=1) * (1.0 - fraction) + jnp.take(knots, knot_index + 1, axis=1) * fraction


def enveloped(key, length, top, noise):
    segments = (length + 7) // 8
    signal_envelope = jnp.exp(jax.random.uniform(key, (CHANNELS, segments), jnp.float32, 0.0, math.log(top)))
    signal_envelope = jnp.repeat(signal_envelope, 8, axis=1)[:, :length]
    return noise * signal_envelope


def draw_record(key, part):
    gain = channel_gain(key)
    drift = baseline_drift(key)[:, :TIME]
    key = jax.random.fold_in(key, 1)
    first_key, second_key = jax.random.split(key)
    noise = jax.random.normal(first_key, (CHANNELS, TIME), jnp.float32)
    top = 10.0
    return ((enveloped(second_key, TIME, top, noise) + drift) * gain).astype(jnp.bfloat16)


def draw_tail(key, part):
    gain = channel_gain(key)
    drift = baseline_drift(key)[:, TIME:]
    key = jax.random.fold_in(key, 2)
    first_key, second_key = jax.random.split(key)
    noise = jax.random.normal(first_key, (CHANNELS, CUT - 1), jnp.float32)
    top = 10.0
    return ((enveloped(second_key, CUT - 1, top, noise) + drift) * gain).astype(jnp.bfloat16)


def draw_det_start(key, part):
    key = jax.random.fold_in(key, 7)
    blocks = jnp.arange(DETS, dtype=jnp.int32) // DET_BLK
    starts = (blocks * TS + jax.random.randint(key, (DETS,), 0, TS, jnp.int32)).astype(jnp.int32)
    starts = starts.at[0].set(0)
    starts = starts.at[DETS - 1].set(TIME - 1)
    return starts.astype(jnp.int32)


def draw_det_owner(key, part):
    key = jax.random.fold_in(key, 5)
    slot_total = N_STA * CAP

    def one_block(block_key):
        order_key, favored_key, shuffle_key = jax.random.split(block_key, 3)
        order = jax.random.permutation(order_key, slot_total).astype(jnp.int32)
        favored = jax.random.randint(favored_key, (), 0, N_STA, jnp.int32)
        owner_of = jnp.arange(slot_total, dtype=jnp.int32) // CAP
        scores = jnp.where(owner_of == favored, order - slot_total, order)
        picked = jnp.argsort(scores, stable=True)[:DET_BLK].astype(jnp.int32)
        shuffled = jax.random.permutation(shuffle_key, picked)
        return (shuffled // CAP).astype(jnp.int32)
    block_key_list = jax.vmap(lambda number: jax.random.fold_in(key, number))(jnp.arange(DETS // DET_BLK))
    return jax.vmap(one_block)(block_key_list).reshape(DETS).astype(jnp.int32)


def with_ends(values, stream_key, least, largest):
    extent = values.shape
    place = [jax.random.randint(jax.random.fold_in(stream_key, axis), (), 0, extent[axis]) for axis in range(len(extent))]
    values = values.at[tuple(place)].set(least)
    longest = extent.index(max(extent))
    place[longest] = (place[longest] + 1) % extent[longest]
    return values.at[tuple(place)].set(largest)


def block_scale(rng, dims, cuts, low, top_value):
    factor_of, own = 1.0, jax.random.fold_in(rng, 6)
    for dim, shards_of in cuts:
        steps = jnp.exp(jax.random.uniform(jax.random.fold_in(own, dim), (shards_of,), jnp.float32, low / len(cuts), top_value / len(cuts)))
        factor_of = factor_of * jnp.repeat(steps, dims[dim] // shards_of).reshape([-1 if axis == dim else 1 for axis in range(len(dims))])
    return factor_of


def bell_draw(rng, dims, scale, most, shards=(), kind=jnp.bfloat16):
    drawn = jax.random.normal(rng, dims, jnp.float32) * scale
    if len(shards) > 0:
        drawn = block_scale(rng, dims, shards, -0.22, 0.18) * drawn
    return jnp.clip(drawn, min=-most, max=most).astype(kind)


def setup_inputs(seed: int = 0) -> dict:
    keys = jax.random.split(jax.random.key(seed), 9)
    return {
        "record": draw_record(jax.random.fold_in(keys[8], 71), 0),
        "tail": draw_tail(jax.random.fold_in(keys[8], 71), 0),
        "templates": bell_draw(keys[2], (CHANNELS, L, K), 1.0, 6.0, ((0, 8),)),
        "live": with_ends((jax.random.randint(keys[3], (CHANNELS,), 0, 8) < 7).astype(jnp.int32), jax.random.fold_in(keys[3], 1), 0, 1),
        "det_template": with_ends(jax.random.randint(keys[4], (DETS,), 0, K), jax.random.fold_in(keys[4], 1), 0, K - 1).astype(jnp.int32),
        "det_start": draw_det_start(jax.random.fold_in(keys[8], 71), 0),
        "det_owner": draw_det_owner(jax.random.fold_in(keys[8], 71), 0),
        "det_mask": with_ends((jax.random.randint(keys[7], (DETS, CHANNELS), 0, 4) < 3).astype(jnp.int32), jax.random.fold_in(keys[7], 1), 0, 1),
    }


EPSILON = 1e-06

def normalize(templates):
    values = templates.astype(jnp.float32)
    centred = values - lax.optimization_barrier(jnp.mean(values, axis=1, keepdims=True))
    spread = lax.optimization_barrier(jnp.mean(centred * centred, axis=1, keepdims=True))
    return (centred / jnp.sqrt(templates.shape[1] * (spread + EPSILON))).astype(jnp.bfloat16)

def reference(record, tail, templates, live, det_template, det_start, det_owner, det_mask):
    extended = jnp.concatenate([record, tail], axis=1)
    normed = normalize(templates)
    wide_normalized_trace = normed.astype(jnp.float32)
    windows = TS + NLAG - 1
    offsets = (jnp.arange(L, dtype=jnp.int32)[:, None] + jnp.arange(windows, dtype=jnp.int32)[None, :]).astype(jnp.int32)
    live_wide = live.astype(jnp.float32)

    def per_block(block_index):
        anchor = (block_index * TS).astype(jnp.int32)
        piece = lax.dynamic_slice_in_dim(extended, anchor, TS + CUT - 1, 1)
        unfolded = jnp.take(piece, offsets, axis=1)
        wide = unfolded.astype(jnp.float32)
        window_mean = lax.optimization_barrier(jnp.mean(wide, axis=1))
        window_square = lax.optimization_barrier(jnp.mean(wide * wide, axis=1))
        weight = live_wide[:, None] / jnp.sqrt(L * (window_square - window_mean * window_mean + EPSILON))
        scaled_low = lax.optimization_barrier(((wide[:, :, :TS] - window_mean[:, None, :TS]) * weight[:, None, :TS]).astype(jnp.bfloat16))
        rescaled_trace = scaled_low.astype(jnp.float32)
        block_stack_sum = jnp.einsum('xup,xuw->pw', wide_normalized_trace, rescaled_trace, precision=lax.Precision.HIGHEST)
        first = (block_index * DET_BLK).astype(jnp.int32)
        kinds = lax.dynamic_slice_in_dim(det_template, first, DET_BLK, 0)
        starts = (lax.dynamic_slice_in_dim(det_start, first, DET_BLK, 0) - anchor).astype(jnp.int32)
        chosen_mask = lax.dynamic_slice_in_dim(det_mask, first, DET_BLK, 0).astype(jnp.float32)
        chosen = jnp.take(wide_normalized_trace, kinds, axis=2)
        correlated = jnp.einsum('cld,clw->dcw', chosen, wide, precision=lax.Precision.HIGHEST) * weight[None]
        lagged = jax.vmap(lambda series, begin: lax.dynamic_slice_in_dim(series, begin, NLAG, 1))(correlated, starts)
        values = (lagged * chosen_mask[:, :, None]).astype(jnp.bfloat16)
        return (block_stack_sum, values)
    stacks, values = lax.map(per_block, jnp.arange(N_TM, dtype=jnp.int32))
    stack = jnp.transpose(stacks, (1, 0, 2)).reshape(K, TIME)
    positions = jnp.arange(DETS, dtype=jnp.int32)
    blocks = (positions // DET_BLK).astype(jnp.int32)
    earlier = (blocks[:, None] == blocks[None, :]) & (det_owner[:, None] == det_owner[None, :]) & (positions[None, :] < positions[:, None])
    rank = lax.optimization_barrier(jnp.sum(earlier.astype(jnp.int32), axis=1)).astype(jnp.int32)
    slot = ((blocks * N_STA + det_owner) * CAP + rank).astype(jnp.int32)
    xcorr = jnp.zeros((SLOTS, CHANNELS, NLAG), jnp.bfloat16).at[slot].set(values.reshape(DETS, CHANNELS, NLAG))
    return (stack, xcorr)
```

```python
import functools
import jax
import jax.numpy as jnp
from jax import lax
from jax.experimental import pallas as pl
from jax.experimental.pallas import tpu as pltpu
from jax.sharding import PartitionSpec as P

CAP = 4
EPSILON = 1e-06
GROUP = 4
MESH = pl.DeviceIdType.MESH


def round_up(value, unit):
    return (value + unit - 1) // unit * unit


def compute_kernel(template_len, block_len, lag_count, sta_count,
                   live_ref, kind_ref, start_ref, owner_ref,
                   record_ref, following_ref, mask_ref, templates_ref,
                   part_ref, packed_ref,
                   ext, shifts, mean, weight, total, series, onehot, mask, counts):
    channels = record_ref.shape[0]
    detections = kind_ref.shape[0]
    rows = onehot.shape[0]
    kinds = onehot.shape[1]
    width = ext.shape[1]
    windows = mean.shape[1]
    step = pl.program_id(0)
    tm_index = lax.axis_index("tm")

    @pl.when(step == 0)
    def _():
        border = following_ref.shape[1]
        ext[...] = jnp.zeros_like(ext)
        ext[:, :block_len] = record_ref[...].astype(jnp.float32)
        ext[:, block_len:block_len + border] = following_ref[...].astype(jnp.float32)
        sums = ext[...]
        squares = sums * sums

        def left(x, by):
            return pltpu.roll(x, width - by, 1)

        def window_sum(x):
            out, offset, span = None, 0, 1
            powers = []
            while span <= template_len:
                powers.append((span, x))
                if span * 2 <= template_len:
                    x = x + left(x, span)
                span *= 2
            for span, value in reversed(powers):
                if template_len & span:
                    value = value if offset == 0 else left(value, offset)
                    out = value if out is None else out + value
                    offset += span
            return out[:, :windows]

        for r in range(8):
            moved = sums if r == 0 else left(sums, r)
            for j in range(width // 128):
                shifts[j, pl.ds(r, channels, stride=8), :] = moved[:, j * 128:j * 128 + 128]
        average = window_sum(sums) * (1.0 / template_len)
        square = window_sum(squares) * (1.0 / template_len)
        row = lax.broadcasted_iota(jnp.int32, (channels, windows), 0)
        alive = jnp.zeros((channels, windows), jnp.float32)
        for c in range(channels):
            alive = jnp.where(row == c, live_ref[c].astype(jnp.float32), alive)
        mean[...] = average
        weight[...] = alive / jnp.sqrt(template_len * (square - average * average + EPSILON))
        total[...] = jnp.zeros_like(total)
        packed_ref[...] = jnp.zeros_like(packed_ref)
        row = lax.broadcasted_iota(jnp.int32, (rows, kinds), 0)
        column = lax.broadcasted_iota(jnp.int32, (rows, kinds), 1)
        chosen = jnp.full((rows, kinds), -1, jnp.int32)
        for d in range(detections):
            chosen = jnp.where(row == d, kind_ref[d], chosen)
        onehot[...] = (chosen == column).astype(jnp.float32).astype(jnp.bfloat16)
        mask[...] = jnp.zeros_like(mask)
        mask[:detections, :] = mask_ref[...].astype(jnp.float32)

    all_normed, all_scaled = [], []
    for g in range(GROUP):
        c = step * GROUP + g
        values = templates_ref[g].astype(jnp.float32)
        centred = values - jnp.mean(values, axis=0, keepdims=True)
        spread = jnp.mean(centred * centred, axis=0, keepdims=True)
        normed = (centred * lax.rsqrt(template_len * (spread + EPSILON))).astype(jnp.bfloat16)
        trace = jnp.concatenate(
            [shifts[j, pl.ds(pl.multiple_of(c * 8, 8), 8), :] for j in range(width // 128)], axis=1)
        hankel = jnp.concatenate(
            [trace] + [pltpu.roll(trace, width - 8 * s, 1) for s in range(1, 16)], axis=0)
        pieces = []
        for low in range(0, template_len, 128):
            count = min(128, template_len - low)
            pieces.append(hankel[:count, low:low + windows])
        unfolded = jnp.concatenate(pieces, axis=0)
        weights = weight[pl.ds(c, 1), :]
        scaled = ((unfolded[:, :block_len] - mean[pl.ds(c, 1), :block_len])
                  * weights[:, :block_len]).astype(jnp.bfloat16)
        all_normed.append(normed)
        all_scaled.append(scaled)
        picked = lax.dot_general(onehot[...], normed, (((1,), (1,)), ((), ())),
                                 preferred_element_type=jnp.float32).astype(jnp.bfloat16)
        found = jnp.dot(picked, unfolded.astype(jnp.bfloat16), preferred_element_type=jnp.float32)
        lane = lax.broadcasted_iota(jnp.int32, mask.shape, 1)
        used = jnp.sum(jnp.where(lane == c, mask[...], 0.0), axis=1, keepdims=True)
        found = found * weights * used
        for j in range(windows // 128):
            series[j, pl.ds(pl.multiple_of(c * rows, rows), rows), :] = found[:, j * 128:j * 128 + 128]
    total[...] += lax.dot_general(
        jnp.concatenate(all_normed, axis=0), jnp.concatenate(all_scaled, axis=0),
        (((0,), (0,)), ((), ())), preferred_element_type=jnp.float32)

    @pl.when(step == pl.num_programs(0) - 1)
    def _():
        part_ref[...] = total[...].astype(jnp.bfloat16)
        for s in range(sta_count):
            counts[s] = 0
        span = lag_count + 128

        def place(d, carry):
            owner = owner_ref[d]
            rank = counts[owner]
            counts[owner] = rank + 1
            start = start_ref[d] - tm_index * block_len
            base = start // 128
            piece = jnp.concatenate(
                [series[base + j, pl.ds(d, channels, stride=rows), :] for j in range(span // 128)], axis=1)
            moved = pltpu.roll(piece, lax.rem(span - (start - base * 128), span), 1)
            packed_ref[owner * CAP + rank] = moved[:, :lag_count].astype(jnp.bfloat16)
            return carry

        lax.fori_loop(0, detections, place, 0)


def exchange_kernel(sta_count, part_ref, packed_ref, stack_ref, xcorr_ref, landed,
                    send_sem, recv_sem, send_sem2, recv_sem2, own_sem):
    me = lax.axis_index("sta")
    tm = lax.axis_index("tm")
    own_rows = stack_ref.shape[0]
    channels = packed_ref.shape[1]
    barrier = pltpu.get_barrier_semaphore()
    for off in range(1, sta_count):
        pl.semaphore_signal(barrier, inc=1, device_id=(tm, lax.rem(me + off, sta_count)), device_id_type=MESH)
    pl.semaphore_wait(barrier, sta_count - 1)
    mine = xcorr_ref.at[:, pl.ds(pl.multiple_of(me * channels, channels), channels), :]
    copies = []
    for off in range(1, sta_count):
        peer = lax.rem(me + off, sta_count)
        copy = pltpu.make_async_remote_copy(
            src_ref=part_ref.at[pl.ds(pl.multiple_of(peer * own_rows, own_rows), own_rows), :],
            dst_ref=landed.at[off - 1], send_sem=send_sem.at[off - 1], recv_sem=recv_sem.at[off - 1],
            device_id=(tm, peer), device_id_type=MESH)
        copy.start()
        copies.append(copy)
    others = []
    for off in range(1, sta_count):
        peer = lax.rem(me + off, sta_count)
        copy = pltpu.make_async_remote_copy(
            src_ref=packed_ref.at[pl.ds(peer * CAP, CAP)],
            dst_ref=mine, send_sem=send_sem2.at[off - 1], recv_sem=recv_sem2.at[off - 1],
            device_id=(tm, peer), device_id_type=MESH)
        copy.start()
        others.append(copy)
    own = pltpu.make_async_copy(packed_ref.at[pl.ds(me * CAP, CAP)], mine, own_sem)
    own.start()
    summed = part_ref[pl.ds(pl.multiple_of(me * own_rows, own_rows), own_rows), :].astype(jnp.float32)
    for off in range(1, sta_count):
        copies[off - 1].wait()
        summed += landed[off - 1].astype(jnp.float32)
    stack_ref[...] = summed
    own.wait()
    for copy in others:
        copy.wait()


def local(record, tail, templates, live, det_template, det_start, det_owner, det_mask):
    channels, block_len = record.shape
    template_len, template_count = templates.shape[1:]
    border_pad = tail.shape[1]
    lag_count = border_pad - template_len + 2
    sta_count = lax.axis_size("sta")
    tm_count = lax.axis_size("tm")
    detections = det_owner.shape[0]
    rows = round_up(detections, 16)
    windows = block_len + lag_count
    width = round_up(block_len + border_pad + 1, 128)
    following = lax.ppermute(record[:, :border_pad], "tm", [(s, s - 1) for s in range(1, tm_count)])
    following = jnp.where(lax.axis_index("tm") == tm_count - 1, tail, following)
    smem = pl.BlockSpec(memory_space=pltpu.SMEM)
    vmem = pl.BlockSpec(memory_space=pltpu.VMEM)
    part, packed = pl.pallas_call(
        functools.partial(compute_kernel, template_len, block_len, lag_count, sta_count),
        grid=(channels // GROUP,),
        in_specs=[smem] * 4 + [vmem] * 3 + [
            pl.BlockSpec((GROUP, template_len, template_count), lambda i: (i, 0, 0))],
        out_specs=[vmem, vmem],
        out_shape=[
            jax.ShapeDtypeStruct((template_count, block_len), jnp.bfloat16),
            jax.ShapeDtypeStruct((sta_count * CAP, channels, lag_count), jnp.bfloat16)],
        scratch_shapes=[
            pltpu.VMEM((channels, width), jnp.float32),
            pltpu.VMEM((width // 128, channels * 8, 128), jnp.float32),
            pltpu.VMEM((channels, windows), jnp.float32),
            pltpu.VMEM((channels, windows), jnp.float32),
            pltpu.VMEM((template_count, block_len), jnp.float32),
            pltpu.VMEM((windows // 128, channels * rows, 128), jnp.float32),
            pltpu.VMEM((rows, template_count), jnp.bfloat16),
            pltpu.VMEM((rows, channels), jnp.float32),
            pltpu.SMEM((sta_count,), jnp.int32)],
        compiler_params=pltpu.CompilerParams(vmem_limit_bytes=48 * 1024 * 1024),
    )(live, det_template, det_start, det_owner, record, following, det_mask, templates)
    own_rows = template_count // sta_count
    dma = pltpu.SemaphoreType.DMA((sta_count - 1,))
    stack, xcorr = pl.pallas_call(
        functools.partial(exchange_kernel, sta_count),
        in_specs=[vmem, vmem],
        out_specs=[vmem, vmem],
        out_shape=[
            jax.ShapeDtypeStruct((own_rows, block_len), jnp.float32),
            jax.ShapeDtypeStruct((CAP, sta_count * channels, lag_count), jnp.bfloat16)],
        scratch_shapes=[
            pltpu.VMEM((sta_count - 1, own_rows, block_len), jnp.bfloat16),
            dma, dma, dma, dma, pltpu.SemaphoreType.DMA],
        compiler_params=pltpu.CompilerParams(
            collective_id=0, has_side_effects=True, vmem_limit_bytes=48 * 1024 * 1024),
    )(part, packed)
    return stack, xcorr


def solution(mesh):
    in_specs = (
        P("sta", "tm"),
        P("sta", None),
        P("sta", None, None),
        P("sta"),
        P("tm"),
        P("tm"),
        P("tm"),
        P("tm", "sta"),
    )
    out_specs = (P("sta", "tm"), P(("tm", "sta"), None, None))
    return jax.shard_map(local, mesh=mesh, in_specs=in_specs, out_specs=out_specs, check_vma=False)
```

```python
import functools
import jax
import jax.numpy as jnp
from jax import lax
from jax.experimental import pallas as pl
from jax.experimental.pallas import tpu as pltpu
from jax.sharding import PartitionSpec as P

CAP = 4
EPSILON = 1e-06
CHUNKS = 4
PAIR = 2
MESH = pl.DeviceIdType.MESH


def round_up(value, unit):
    return (value + unit - 1) // unit * unit


def kernel(lag_count, sta_count, tm_count,
           record_hbm, tail_hbm, templates_hbm, live_hbm, kind_hbm, start_hbm, owner_hbm, mask_hbm,
           stack_ref, xcorr_ref,
           record, tail, templates, live, kinds, starts, owners, used_raw, halo,
           normed, scaled, ext, shifts, mean, weight, series, values, onehot, mask, packed,
           block, kept, sibling_out, sibling_in, pair_out, landed,
           load_sem, template_sem, halo_sem, xs_sem, xr_sem, own_sem, ss_sem, sr_sem, ps_sem, pr_sem):
    channels, block_len = record.shape
    template_len, template_count = templates.shape[1:]
    border = tail.shape[1]
    detections = mask_hbm.shape[0]
    rows = onehot.shape[0]
    width = ext.shape[1]
    windows = mean.shape[1]
    chips = sta_count // 2
    own_rows = stack_ref.shape[0]
    tm = lax.axis_index("tm")
    me = lax.axis_index("sta")
    chip = me // 2
    core = lax.rem(me, 2)
    sibling = me + 1 - 2 * core

    loads = [pltpu.make_async_copy(src, dst, load_sem.at[i]) for i, (src, dst) in enumerate((
        (record_hbm, record), (tail_hbm, tail), (live_hbm, live), (kind_hbm, kinds),
        (start_hbm, starts), (owner_hbm, owners), (mask_hbm, used_raw)))]
    for load in loads:
        load.start()
    per = channels // CHUNKS
    template_loads = [pltpu.make_async_copy(
        templates_hbm.at[pl.ds(i * per, per)], templates.at[pl.ds(i * per, per)], template_sem.at[i])
        for i in range(CHUNKS)]
    for load in template_loads:
        load.start()

    barrier = pltpu.get_barrier_semaphore()
    for off in range(1, sta_count):
        pl.semaphore_signal(barrier, inc=1, device_id=(tm, lax.rem(me + off, sta_count)), device_id_type=MESH)

    @pl.when(tm < tm_count - 1)
    def _():
        pl.semaphore_signal(barrier, inc=1, device_id=(tm + 1, me), device_id_type=MESH)

    pl.semaphore_wait(barrier, sta_count - 1 + (tm > 0).astype(jnp.int32))
    halo_copy = pltpu.make_async_remote_copy(
        src_ref=record_hbm.at[:, pl.ds(0, halo.shape[1])], dst_ref=halo,
        send_sem=halo_sem.at[0], recv_sem=halo_sem.at[1],
        device_id=(tm - 1, me), device_id_type=MESH)

    @pl.when(tm > 0)
    def _():
        halo_copy.start()

    for load in loads:
        load.wait()
    row = lax.broadcasted_iota(jnp.int32, (rows, template_count), 0)
    column = lax.broadcasted_iota(jnp.int32, (rows, template_count), 1)
    chosen = jnp.full((rows, template_count), -1, jnp.int32)
    for d in range(detections):
        chosen = jnp.where(row == d, kinds[d], chosen)
    onehot[...] = (chosen == column).astype(jnp.float32).astype(jnp.bfloat16)
    mask[...] = jnp.zeros_like(mask)
    mask[:detections, :] = used_raw[...].astype(jnp.float32)

    for i in range(CHUNKS):
        template_loads[i].wait()

        def normalize(c, carry):
            wide = templates[c].astype(jnp.float32)
            centred = wide - jnp.mean(wide, axis=0, keepdims=True)
            spread = jnp.mean(centred * centred, axis=0, keepdims=True)
            normed[c] = (centred * lax.rsqrt(template_len * (spread + EPSILON))).astype(jnp.bfloat16)
            return carry

        lax.fori_loop(i * per, (i + 1) * per, normalize, 0)

    last = tm == tm_count - 1

    @pl.when(jnp.logical_not(last))
    def _():
        halo_copy.wait_recv()
        ext[:, block_len:block_len + border] = halo[:, :border].astype(jnp.float32)

    @pl.when(last)
    def _():
        ext[:, block_len:block_len + border] = tail[...].astype(jnp.float32)

    @pl.when(tm > 0)
    def _():
        halo_copy.wait_send()

    ext[:, :block_len] = record[...].astype(jnp.float32)
    lane = lax.broadcasted_iota(jnp.int32, (channels, width), 1)
    sums = jnp.where(lane < block_len + border, ext[...], 0.0)
    squares = sums * sums

    def left(x, by):
        return pltpu.roll(x, width - by, 1)

    def window_sum(x):
        out, offset, span = None, 0, 1
        powers = []
        while span <= template_len:
            powers.append((span, x))
            if span * 2 <= template_len:
                x = x + left(x, span)
            span *= 2
        for span, value in reversed(powers):
            if template_len & span:
                value = value if offset == 0 else left(value, offset)
                out = value if out is None else out + value
                offset += span
        return out[:, :windows]

    for r in range(8):
        moved = sums if r == 0 else left(sums, r)
        for j in range(width // 128):
            shifts[j, pl.ds(r, channels, stride=8), :] = moved[:, j * 128:j * 128 + 128]
    average = window_sum(sums) * (1.0 / template_len)
    square = window_sum(squares) * (1.0 / template_len)
    row = lax.broadcasted_iota(jnp.int32, (channels, windows), 0)
    alive = jnp.zeros((channels, windows), jnp.float32)
    for c in range(channels):
        alive = jnp.where(row == c, live[c].astype(jnp.float32), alive)
    mean[...] = average
    weight[...] = alive / jnp.sqrt(template_len * (square - average * average + EPSILON))

    def unfold(step, carry):
        for g in range(PAIR):
            c = step * PAIR + g
            trace = jnp.concatenate(
                [shifts[j, pl.ds(pl.multiple_of(c * 8, 8), 8), :] for j in range(width // 128)], axis=1)
            hankel = jnp.concatenate(
                [trace] + [pltpu.roll(trace, width - 8 * s, 1) for s in range(1, 16)], axis=0)
            pieces = []
            for low in range(0, template_len, 128):
                count = min(128, template_len - low)
                pieces.append(hankel[:count, low:low + windows])
            unfolded = jnp.concatenate(pieces, axis=0)
            weights = weight[pl.ds(c, 1), :]
            scaled[c] = ((unfolded[:, :block_len] - mean[pl.ds(c, 1), :block_len])
                         * weights[:, :block_len]).astype(jnp.bfloat16)
            picked = lax.dot_general(onehot[...], normed[c], (((1,), (1,)), ((), ())),
                                     preferred_element_type=jnp.float32).astype(jnp.bfloat16)
            found = jnp.dot(picked, unfolded.astype(jnp.bfloat16), preferred_element_type=jnp.float32)
            lane = lax.broadcasted_iota(jnp.int32, mask.shape, 1)
            used = jnp.sum(jnp.where(lane == c, mask[...], 0.0), axis=1, keepdims=True)
            found = found * weights * used
            for j in range(windows // 128):
                series[j, pl.ds(pl.multiple_of(c * rows, rows), rows), :] = found[:, j * 128:j * 128 + 128]
        return carry

    lax.fori_loop(0, channels // PAIR, unfold, 0)

    span = lag_count + 128
    values[...] = jnp.zeros_like(values)

    def cut(d, carry):
        start = jnp.clip(starts[d] - tm * block_len, 0, block_len - 1)
        base = lax.shift_right_logical(start, 7)
        piece = jnp.concatenate(
            [series[base + j, pl.ds(d, channels, stride=rows), :] for j in range(span // 128)], axis=1)
        moved = pltpu.roll(piece, span - (start - base * 128), 1)
        values[pl.ds(pl.multiple_of(d * channels, channels), channels), :] = (
            moved[:, :lag_count].astype(jnp.bfloat16))
        return carry

    lax.fori_loop(0, detections, cut, 0)
    columns = values.shape[0]
    earlier = lax.broadcasted_iota(jnp.int32, (rows, columns), 0)
    spot = lax.broadcasted_iota(jnp.int32, (rows, columns), 1)
    now = spot // channels
    by_row = jnp.full((rows, columns), -1, jnp.int32)
    by_column = jnp.full((rows, columns), -2, jnp.int32)
    for d in range(detections):
        by_row = jnp.where(earlier == d, owners[d], by_row)
        by_column = jnp.where(now == d, owners[d], by_column)
    same = jnp.where((by_row == by_column) & (earlier < now), 1.0, 0.0)
    rank = jnp.sum(same, axis=0, keepdims=True).astype(jnp.int32)
    slot = by_column[:1] * CAP + rank
    place = slot * channels + (spot - now * channels)[:1]
    part = CAP * channels
    for off in list(range(1, sta_count)) + [0]:
        peer = lax.rem(me + off, sta_count)
        target = lax.broadcasted_iota(jnp.int32, (part, columns), 0) + peer * part
        putting = (target == place).astype(jnp.float32).astype(jnp.bfloat16)
        filled = jnp.dot(putting, values[...], preferred_element_type=jnp.float32)
        packed[pl.ds(peer * CAP, CAP)] = filled.astype(jnp.bfloat16).reshape(CAP, channels, lag_count)

    mine = xcorr_ref.at[:, pl.ds(pl.multiple_of(me * channels, channels), channels), :]
    sent = []
    for off in range(1, sta_count):
        peer = lax.rem(me + off, sta_count)
        copy = pltpu.make_async_remote_copy(
            src_ref=packed.at[pl.ds(peer * CAP, CAP)], dst_ref=mine,
            send_sem=xs_sem.at[off - 1], recv_sem=xr_sem.at[off - 1],
            device_id=(tm, peer), device_id_type=MESH)
        copy.start()
        sent.append(copy)
    own = pltpu.make_async_copy(packed.at[pl.ds(me * CAP, CAP)], mine, own_sem)
    own.start()

    count = block.shape[0]
    blocks = template_count // count
    each = count // (2 * own_rows)

    def to_sibling(q):
        return pltpu.make_async_remote_copy(
            src_ref=sibling_out.at[q], dst_ref=sibling_in.at[q],
            send_sem=ss_sem.at[q], recv_sem=sr_sem.at[q],
            device_id=(tm, sibling), device_id_type=MESH)

    def to_chip(off):
        return pltpu.make_async_remote_copy(
            src_ref=pair_out.at[off], dst_ref=landed.at[off],
            send_sem=ps_sem.at[off], recv_sem=pr_sem.at[off],
            device_id=(tm, lax.rem(chip + off, chips) * 2 + core), device_id_type=MESH)

    def pass_on(b):
        for j in range(each):
            q = b * each + j
            to_sibling(q).wait_recv()
            off = lax.rem(q - chip + chips, chips)

            @pl.when(off > 0)
            def _():
                pair_out[off] = (kept[q] + sibling_in[q].astype(jnp.float32)).astype(jnp.bfloat16)
                to_chip(off).start()

    flat = channels * template_len
    for i in range(blocks):
        b = lax.rem(chip // each + 1 + i, blocks)
        block[...] = lax.dot_general(
            normed[:, :, pl.ds(pl.multiple_of(b * count, count), count)].reshape(flat, count),
            scaled[...].reshape(flat, block_len), (((0,), (0,)), ((), ())),
            preferred_element_type=jnp.float32)
        for j in range(each):
            q = b * each + j
            low = (2 * j + core) * own_rows
            other = (2 * j + 1 - core) * own_rows
            sibling_out[q] = block[pl.ds(pl.multiple_of(other, 8), own_rows), :].astype(jnp.bfloat16)
            to_sibling(q).start()
            kept[q] = block[pl.ds(pl.multiple_of(low, 8), own_rows), :]
        if i > 0:
            pass_on(lax.rem(chip // each + i, blocks))
    pass_on(lax.rem(chip // each + blocks, blocks))
    result = kept[chip] + sibling_in[chip].astype(jnp.float32)
    for off in range(1, chips):
        to_chip(off).wait()
        result += landed[off].astype(jnp.float32)
    stack_ref[...] = result
    for q in range(chips):
        to_sibling(q).wait_send()
    own.wait()
    for copy in sent:
        copy.wait()


def local(record, tail, templates, live, det_template, det_start, det_owner, det_mask):
    channels, block_len = record.shape
    template_len, template_count = templates.shape[1:]
    border = tail.shape[1]
    lag_count = border - template_len + 2
    sta_count = lax.axis_size("sta")
    tm_count = lax.axis_size("tm")
    detections = det_owner.shape[0]
    rows = round_up(detections, 16)
    windows = block_len + lag_count
    width = round_up(block_len + border + 1, 128)
    own_rows = template_count // sta_count
    chips = sta_count // 2
    count = max(128, 2 * own_rows)
    bf16, f32, i32 = jnp.bfloat16, jnp.float32, jnp.int32
    dma = pltpu.SemaphoreType.DMA
    anywhere = pl.BlockSpec(memory_space=pl.ANY)
    vmem = pl.BlockSpec(memory_space=pltpu.VMEM)
    return pl.pallas_call(
        functools.partial(kernel, lag_count, sta_count, tm_count),
        in_specs=[anywhere] * 8,
        out_specs=[vmem, vmem],
        out_shape=[
            jax.ShapeDtypeStruct((own_rows, block_len), f32),
            jax.ShapeDtypeStruct((CAP, sta_count * channels, lag_count), bf16)],
        scratch_shapes=[
            pltpu.VMEM(record.shape, bf16),
            pltpu.VMEM(tail.shape, bf16),
            pltpu.VMEM(templates.shape, bf16),
            pltpu.SMEM(live.shape, i32),
            pltpu.SMEM(det_template.shape, i32),
            pltpu.SMEM(det_start.shape, i32),
            pltpu.SMEM(det_owner.shape, i32),
            pltpu.VMEM(det_mask.shape, i32),
            pltpu.VMEM((channels, round_up(border, 128)), bf16),
            pltpu.VMEM(templates.shape, bf16),
            pltpu.VMEM((channels, template_len, block_len), bf16),
            pltpu.VMEM((channels, width), f32),
            pltpu.VMEM((width // 128, channels * 8, 128), f32),
            pltpu.VMEM((channels, windows), f32),
            pltpu.VMEM((channels, windows), f32),
            pltpu.VMEM((windows // 128, channels * rows, 128), f32),
            pltpu.VMEM((rows * channels, lag_count), bf16),
            pltpu.VMEM((rows, template_count), bf16),
            pltpu.VMEM((rows, channels), f32),
            pltpu.VMEM((sta_count * CAP, channels, lag_count), bf16),
            pltpu.VMEM((count, block_len), f32),
            pltpu.VMEM((chips, own_rows, block_len), f32),
            pltpu.VMEM((chips, own_rows, block_len), bf16),
            pltpu.VMEM((chips, own_rows, block_len), bf16),
            pltpu.VMEM((chips, own_rows, block_len), bf16),
            pltpu.VMEM((chips, own_rows, block_len), bf16),
            dma((7,)), dma((CHUNKS,)), dma((2,)),
            dma((sta_count - 1,)), dma((sta_count - 1,)), dma,
            dma((chips,)), dma((chips,)), dma((chips,)), dma((chips,))],
        compiler_params=pltpu.CompilerParams(
            collective_id=0, has_side_effects=True, vmem_limit_bytes=56 * 1024 * 1024),
    )(record, tail, templates, live, det_template, det_start, det_owner, det_mask)


def solution(mesh):
    in_specs = (
        P("sta", "tm"),
        P("sta", None),
        P("sta", None, None),
        P("sta"),
        P("tm"),
        P("tm"),
        P("tm"),
        P("tm", "sta"),
    )
    out_specs = (P("sta", "tm"), P(("tm", "sta"), None, None))
    return jax.shard_map(local, mesh=mesh, in_specs=in_specs, out_specs=out_specs, check_vma=False)
```

```python
import functools
import jax
import jax.numpy as jnp
from jax import lax
from jax.experimental import pallas as pl
from jax.experimental.pallas import tpu as pltpu
from jax.sharding import PartitionSpec as P

CAP = 4
EPSILON = 1e-06
CHUNKS = 4
PAIR = 2
MESH = pl.DeviceIdType.MESH


def round_up(value, unit):
    return (value + unit - 1) // unit * unit


def kernel(lag_count, sta_count, tm_count,
           record_hbm, tail_hbm, templates_hbm, live_hbm, kind_hbm, start_hbm, owner_hbm, mask_hbm,
           stack_ref, xcorr_ref,
           record, tail, templates, live, kinds, starts, owners, used_raw, halo,
           normed, scaled, ext, shifts, mean, weight, unfolded, picks, series, values, onehot, mask, packed,
           block, kept, sibling_out, sibling_in, pair_out, landed,
           load_sem, template_sem, halo_sem, xs_sem, xr_sem, own_sem, ss_sem, sr_sem, ps_sem, pr_sem):
    channels, block_len = record.shape
    template_len, template_count = templates.shape[1:]
    border = tail.shape[1]
    detections = mask_hbm.shape[0]
    rows = onehot.shape[0]
    width = ext.shape[1]
    windows = mean.shape[1]
    chips = sta_count // 2
    own_rows = stack_ref.shape[0]
    tm = lax.axis_index("tm")
    me = lax.axis_index("sta")
    chip = me // 2
    core = lax.rem(me, 2)
    sibling = me + 1 - 2 * core

    per = channels // CHUNKS
    template_loads = [pltpu.make_async_copy(
        templates_hbm.at[pl.ds(i * per, per)], templates.at[pl.ds(i * per, per)], template_sem.at[i])
        for i in range(CHUNKS)]
    for load in template_loads:
        load.start()

    loads = [pltpu.make_async_copy(src, dst, load_sem.at[i]) for i, (src, dst) in enumerate((
        (record_hbm, record), (tail_hbm, tail), (live_hbm, live), (kind_hbm, kinds),
        (start_hbm, starts), (owner_hbm, owners), (mask_hbm, used_raw)))]
    for load in loads:
        load.start()
    barrier = pltpu.get_barrier_semaphore()
    for off in range(1, sta_count):
        pl.semaphore_signal(barrier, inc=1, device_id=(tm, lax.rem(me + off, sta_count)), device_id_type=MESH)

    @pl.when(tm < tm_count - 1)
    def _():
        pl.semaphore_signal(barrier, inc=1, device_id=(tm + 1, me), device_id_type=MESH)

    for i in range(CHUNKS):
        template_loads[i].wait()

        def normalize(c, carry):
            wide = templates[c].astype(jnp.float32)
            centred = wide - jnp.mean(wide, axis=0, keepdims=True)
            spread = jnp.mean(centred * centred, axis=0, keepdims=True)
            normed[c] = (centred * lax.rsqrt(template_len * (spread + EPSILON))).astype(jnp.bfloat16)
            return carry

        lax.fori_loop(i * per, (i + 1) * per, normalize, 0)
        if i == 0:
            pl.semaphore_wait(barrier, sta_count - 1 + (tm > 0).astype(jnp.int32))
            halo_copy = pltpu.make_async_remote_copy(
                src_ref=record_hbm.at[:, pl.ds(0, halo.shape[1])], dst_ref=halo,
                send_sem=halo_sem.at[0], recv_sem=halo_sem.at[1],
                device_id=(tm - 1, me), device_id_type=MESH)

            @pl.when(tm > 0)
            def _():
                halo_copy.start()


    for load in loads:
        load.wait()
    row = lax.broadcasted_iota(jnp.int32, (rows, template_count), 0)
    column = lax.broadcasted_iota(jnp.int32, (rows, template_count), 1)
    chosen = jnp.full((rows, template_count), -1, jnp.int32)
    for d in range(detections):
        chosen = jnp.where(row == d, kinds[d], chosen)
    onehot[...] = (chosen == column).astype(jnp.float32).astype(jnp.bfloat16)
    mask[...] = jnp.zeros_like(mask)
    mask[:detections, :] = used_raw[...].astype(jnp.float32)

    flat = channels * template_len
    picked = lax.dot_general(onehot[...], normed[...].reshape(flat, template_count), (((1,), (1,)), ((), ())),
                             preferred_element_type=jnp.float32)
    for c in range(channels):
        picks[c] = picked[:, c * template_len:(c + 1) * template_len].astype(jnp.bfloat16)
    last = tm == tm_count - 1

    @pl.when(jnp.logical_not(last))
    def _():
        halo_copy.wait_recv()
        ext[:, block_len:block_len + border] = halo[:, :border].astype(jnp.float32)

    @pl.when(last)
    def _():
        ext[:, block_len:block_len + border] = tail[...].astype(jnp.float32)

    @pl.when(tm > 0)
    def _():
        halo_copy.wait_send()

    ext[:, :block_len] = record[...].astype(jnp.float32)
    lane = lax.broadcasted_iota(jnp.int32, (channels, width), 1)
    sums = jnp.where(lane < block_len + border, ext[...], 0.0)
    squares = sums * sums

    def left(x, by):
        return pltpu.roll(x, width - by, 1)

    def window_sum(x):
        out, offset, span = None, 0, 1
        powers = []
        while span <= template_len:
            powers.append((span, x))
            if span * 2 <= template_len:
                x = x + left(x, span)
            span *= 2
        for span, value in reversed(powers):
            if template_len & span:
                value = value if offset == 0 else left(value, offset)
                out = value if out is None else out + value
                offset += span
        return out[:, :windows]

    for r in range(8):
        moved = sums if r == 0 else left(sums, r)
        for j in range(width // 128):
            shifts[j, pl.ds(r, channels, stride=8), :] = moved[:, j * 128:j * 128 + 128]
    average = window_sum(sums) * (1.0 / template_len)
    square = window_sum(squares) * (1.0 / template_len)
    row = lax.broadcasted_iota(jnp.int32, (channels, windows), 0)
    alive = jnp.zeros((channels, windows), jnp.float32)
    for c in range(channels):
        alive = jnp.where(row == c, live[c].astype(jnp.float32), alive)
    mean[...] = average
    weight[...] = alive / jnp.sqrt(template_len * (square - average * average + EPSILON))

    def unfold(step, carry):
        for g in range(PAIR):
            c = step * PAIR + g
            trace = jnp.concatenate(
                [shifts[j, pl.ds(pl.multiple_of(c * 8, 8), 8), :] for j in range(width // 128)], axis=1)
            weights = weight[pl.ds(c, 1), :block_len]
            average = mean[pl.ds(c, 1), :block_len]
            raw, fine = {}, {}
            for s in range(0, 16, 2):
                upper = trace if s == 0 else pltpu.roll(trace, width - 8 * s, 1)
                both = jnp.concatenate([upper, pltpu.roll(trace, width - 8 * s - 8, 1)], axis=0)
                for low in range(0, template_len, 128):
                    first = low + 8 * s
                    used = min(16, template_len - first)
                    if used > 0:
                        piece = both[:used, low:low + windows]
                        raw[first] = piece.astype(jnp.bfloat16)
                        fine[first] = ((piece[:, :block_len] - average) * weights).astype(jnp.bfloat16)
            order = sorted(raw)
            unfolded[c] = jnp.concatenate([raw[k] for k in order], axis=0)
            scaled[c] = jnp.concatenate([fine[k] for k in order], axis=0)
        return carry

    lax.fori_loop(0, channels // PAIR, unfold, 0)

    count = block.shape[0]
    blocks = template_count // count
    each = count // (2 * own_rows)

    def to_sibling(q):
        return pltpu.make_async_remote_copy(
            src_ref=sibling_out.at[q], dst_ref=sibling_in.at[q],
            send_sem=ss_sem.at[q], recv_sem=sr_sem.at[q],
            device_id=(tm, sibling), device_id_type=MESH)

    def to_chip(off):
        return pltpu.make_async_remote_copy(
            src_ref=pair_out.at[off], dst_ref=landed.at[off],
            send_sem=ps_sem.at[off], recv_sem=pr_sem.at[off],
            device_id=(tm, lax.rem(chip + off, chips) * 2 + core), device_id_type=MESH)

    def pass_on(b):
        for j in range(each):
            q = b * each + j
            to_sibling(q).wait_recv()
            off = lax.rem(q - chip + chips, chips)

            @pl.when(off > 0)
            def _():
                pair_out[off] = (kept[q] + sibling_in[q].astype(jnp.float32)).astype(jnp.bfloat16)
                to_chip(off).start()

    home = chip // each

    def nth(i):
        flip, out, bit = blocks - 1 - i, 0, 1
        while bit < blocks:
            digit = lax.rem(home // bit, 2)
            out = out + bit * (1 - digit if flip & bit else digit)
            bit *= 2
        return out

    for i in range(blocks):
        b = nth(i)
        if i == blocks - 1:
            span = lag_count + 128
            values[...] = jnp.zeros_like(values)

            def find(step, carry):
                for g in range(4):
                    c = step * 4 + g
                    found = jnp.dot(picks[c], unfolded[c], preferred_element_type=jnp.float32)
                    lane = lax.broadcasted_iota(jnp.int32, mask.shape, 1)
                    used = jnp.sum(jnp.where(lane == c, mask[...], 0.0), axis=1, keepdims=True)
                    found = found * weight[pl.ds(c, 1), :] * used
                    for j in range(windows // 128):
                        series[j, pl.ds(pl.multiple_of(c * rows, rows), rows), :] = found[:, j * 128:j * 128 + 128]
                return carry

            lax.fori_loop(0, channels // 4, find, 0)
            pass_on(nth(i - 1))

            def cut(d):
                start = jnp.clip(starts[d] - tm * block_len, 0, block_len - 1)
                base = lax.shift_right_logical(start, 7)
                piece = jnp.concatenate(
                    [series[base + j, pl.ds(d, channels, stride=rows), :] for j in range(span // 128)], axis=1)
                moved = pltpu.roll(piece, span - (start - base * 128), 1)
                values[pl.ds(pl.multiple_of(d * channels, channels), channels), :] = (
                    moved[:, :lag_count].astype(jnp.bfloat16))

            run = max(n for n in range(1, 9) if detections % n == 0)

            def cut_some(step, carry):
                for g in range(run):
                    cut(step * run + g)
                return carry

            lax.fori_loop(0, detections // run, cut_some, 0)
            columns = values.shape[0]
            earlier = lax.broadcasted_iota(jnp.int32, (rows, columns), 0)
            spot = lax.broadcasted_iota(jnp.int32, (rows, columns), 1)
            now = spot // channels
            by_row = jnp.full((rows, columns), -1, jnp.int32)
            by_column = jnp.full((rows, columns), -2, jnp.int32)
            for d in range(detections):
                by_row = jnp.where(earlier == d, owners[d], by_row)
                by_column = jnp.where(now == d, owners[d], by_column)
            same = jnp.where((by_row == by_column) & (earlier < now), 1.0, 0.0)
            rank = jnp.sum(same, axis=0, keepdims=True).astype(jnp.int32)
            slot = by_column[:1] * CAP + rank
            place = slot * channels + (spot - now * channels)[:1]
            part = CAP * channels
            for off in list(range(1, sta_count)) + [0]:
                peer = lax.rem(me + off, sta_count)
                target = lax.broadcasted_iota(jnp.int32, (part, columns), 0) + peer * part
                putting = (target == place).astype(jnp.float32).astype(jnp.bfloat16)
                filled = jnp.dot(putting, values[...], preferred_element_type=jnp.float32)
                packed[pl.ds(peer * CAP, CAP)] = filled.astype(jnp.bfloat16).reshape(CAP, channels, lag_count)

            mine = xcorr_ref.at[:, pl.ds(pl.multiple_of(me * channels, channels), channels), :]
            sent = []
            for off in range(1, sta_count):
                peer = lax.rem(me + off, sta_count)
                copy = pltpu.make_async_remote_copy(
                    src_ref=packed.at[pl.ds(peer * CAP, CAP)], dst_ref=mine,
                    send_sem=xs_sem.at[off - 1], recv_sem=xr_sem.at[off - 1],
                    device_id=(tm, peer), device_id_type=MESH)
                copy.start()
                sent.append(copy)
            own = pltpu.make_async_copy(packed.at[pl.ds(me * CAP, CAP)], mine, own_sem)
            own.start()

        block[...] = lax.dot_general(
            normed[:, :, pl.ds(pl.multiple_of(b * count, count), count)].reshape(flat, count),
            scaled[...].reshape(flat, block_len), (((0,), (0,)), ((), ())),
            preferred_element_type=jnp.float32)
        for j in range(each):
            q = b * each + j
            low = (2 * j + core) * own_rows
            other = (2 * j + 1 - core) * own_rows
            sibling_out[q] = block[pl.ds(pl.multiple_of(other, 8), own_rows), :].astype(jnp.bfloat16)
            to_sibling(q).start()
            kept[q] = block[pl.ds(pl.multiple_of(low, 8), own_rows), :]
        if 0 < i < blocks - 1:
            pass_on(nth(i - 1))
    pass_on(nth(blocks - 1))
    result = kept[chip] + sibling_in[chip].astype(jnp.float32)
    for off in range(1, chips):
        to_chip(off).wait()
        result += landed[off].astype(jnp.float32)
    stack_ref[...] = result
    for q in range(chips):
        to_sibling(q).wait_send()
    own.wait()
    for copy in sent:
        copy.wait()


def local(record, tail, templates, live, det_template, det_start, det_owner, det_mask):
    channels, block_len = record.shape
    template_len, template_count = templates.shape[1:]
    border = tail.shape[1]
    lag_count = border - template_len + 2
    sta_count = lax.axis_size("sta")
    tm_count = lax.axis_size("tm")
    detections = det_owner.shape[0]
    rows = round_up(detections, 16)
    windows = block_len + lag_count
    width = round_up(block_len + border + 1, 128)
    own_rows = template_count // sta_count
    chips = sta_count // 2
    count = max(128, 2 * own_rows)
    bf16, f32, i32 = jnp.bfloat16, jnp.float32, jnp.int32
    dma = pltpu.SemaphoreType.DMA
    anywhere = pl.BlockSpec(memory_space=pl.ANY)
    vmem = pl.BlockSpec(memory_space=pltpu.VMEM)
    return pl.pallas_call(
        functools.partial(kernel, lag_count, sta_count, tm_count),
        in_specs=[anywhere] * 8,
        out_specs=[vmem, vmem],
        out_shape=[
            jax.ShapeDtypeStruct((own_rows, block_len), f32),
            jax.ShapeDtypeStruct((CAP, sta_count * channels, lag_count), bf16)],
        scratch_shapes=[
            pltpu.VMEM(record.shape, bf16),
            pltpu.VMEM(tail.shape, bf16),
            pltpu.VMEM(templates.shape, bf16),
            pltpu.SMEM(live.shape, i32),
            pltpu.SMEM(det_template.shape, i32),
            pltpu.SMEM(det_start.shape, i32),
            pltpu.SMEM(det_owner.shape, i32),
            pltpu.VMEM(det_mask.shape, i32),
            pltpu.VMEM((channels, round_up(border, 128)), bf16),
            pltpu.VMEM(templates.shape, bf16),
            pltpu.VMEM((channels, template_len, block_len), bf16),
            pltpu.VMEM((channels, width), f32),
            pltpu.VMEM((width // 128, channels * 8, 128), f32),
            pltpu.VMEM((channels, windows), f32),
            pltpu.VMEM((channels, windows), f32),
            pltpu.VMEM((channels, template_len, windows), bf16),
            pltpu.VMEM((channels, rows, template_len), bf16),
            pltpu.VMEM((windows // 128, channels * rows, 128), f32),
            pltpu.VMEM((rows * channels, lag_count), bf16),
            pltpu.VMEM((rows, template_count), bf16),
            pltpu.VMEM((rows, channels), f32),
            pltpu.VMEM((sta_count * CAP, channels, lag_count), bf16),
            pltpu.VMEM((count, block_len), f32),
            pltpu.VMEM((chips, own_rows, block_len), f32),
            pltpu.VMEM((chips, own_rows, block_len), bf16),
            pltpu.VMEM((chips, own_rows, block_len), bf16),
            pltpu.VMEM((chips, own_rows, block_len), bf16),
            pltpu.VMEM((chips, own_rows, block_len), bf16),
            dma((7,)), dma((CHUNKS,)), dma((2,)),
            dma((sta_count - 1,)), dma((sta_count - 1,)), dma,
            dma((chips,)), dma((chips,)), dma((chips,)), dma((chips,))],
        compiler_params=pltpu.CompilerParams(
            collective_id=0, has_side_effects=True, vmem_limit_bytes=56 * 1024 * 1024),
    )(record, tail, templates, live, det_template, det_start, det_owner, det_mask)


def solution(mesh):
    in_specs = (
        P("sta", "tm"),
        P("sta", None),
        P("sta", None, None),
        P("sta"),
        P("tm"),
        P("tm"),
        P("tm"),
        P("tm", "sta"),
    )
    out_specs = (P("sta", "tm"), P(("tm", "sta"), None, None))
    return jax.shard_map(local, mesh=mesh, in_specs=in_specs, out_specs=out_specs, check_vma=False)
```

```python
import functools
import jax
import jax.numpy as jnp
from jax import lax
from jax.experimental import pallas as pl
from jax.experimental.pallas import tpu as pltpu
from jax.sharding import PartitionSpec as P

CAP = 4
EPSILON = 1e-06
CHUNKS = 4
PAIR = 2
MESH = pl.DeviceIdType.MESH


def round_up(value, unit):
    return (value + unit - 1) // unit * unit


def kernel(lag_count, sta_count, tm_count,
           record_hbm, tail_hbm, templates_hbm, live_hbm, kind_hbm, start_hbm, owner_hbm, mask_hbm,
           stack_ref, xcorr_ref,
           record, tail, templates, live, kinds, starts, owners, used_raw, halo,
           normed, scaled, ext, shifts, mean, weight, unfolded, picks, series, values, onehot, mask, packed,
           block, kept, sibling_out, sibling_in, pair_out, landed,
           load_sem, template_sem, halo_sem, xs_sem, xr_sem, own_sem, ss_sem, sr_sem, ps_sem, pr_sem):
    channels, block_len = record.shape
    template_len, template_count = templates.shape[1:]
    border = tail.shape[1]
    detections = mask_hbm.shape[0]
    rows = onehot.shape[0]
    width = ext.shape[1]
    windows = mean.shape[1]
    chips = sta_count // 2
    own_rows = stack_ref.shape[0]
    tm = lax.axis_index("tm")
    me = lax.axis_index("sta")
    chip = me // 2
    core = lax.rem(me, 2)
    sibling = me + 1 - 2 * core

    per = channels // CHUNKS
    template_loads = [pltpu.make_async_copy(
        templates_hbm.at[pl.ds(i * per, per)], templates.at[pl.ds(i * per, per)], template_sem.at[i])
        for i in range(CHUNKS)]
    for load in template_loads:
        load.start()

    loads = [pltpu.make_async_copy(src, dst, load_sem.at[i]) for i, (src, dst) in enumerate((
        (record_hbm, record), (tail_hbm, tail), (live_hbm, live), (kind_hbm, kinds),
        (start_hbm, starts), (owner_hbm, owners), (mask_hbm, used_raw)))]
    for load in loads:
        load.start()
    barrier = pltpu.get_barrier_semaphore()
    for off in range(1, sta_count):
        pl.semaphore_signal(barrier, inc=1, device_id=(tm, lax.rem(me + off, sta_count)), device_id_type=MESH)

    @pl.when(tm < tm_count - 1)
    def _():
        pl.semaphore_signal(barrier, inc=1, device_id=(tm + 1, me), device_id_type=MESH)

    for i in range(CHUNKS):
        template_loads[i].wait()

        def normalize(c, carry):
            wide = templates[c].astype(jnp.float32)
            centred = wide - jnp.mean(wide, axis=0, keepdims=True)
            spread = jnp.mean(centred * centred, axis=0, keepdims=True)
            normed[c] = (centred * lax.rsqrt(template_len * (spread + EPSILON))).astype(jnp.bfloat16)
            return carry

        lax.fori_loop(i * per, (i + 1) * per, normalize, 0)
        if i == 0:
            pl.semaphore_wait(barrier, sta_count - 1 + (tm > 0).astype(jnp.int32))
            halo_copy = pltpu.make_async_remote_copy(
                src_ref=record_hbm.at[:, pl.ds(0, halo.shape[1])], dst_ref=halo,
                send_sem=halo_sem.at[0], recv_sem=halo_sem.at[1],
                device_id=(tm - 1, me), device_id_type=MESH)

            @pl.when(tm > 0)
            def _():
                halo_copy.start()


    for load in loads:
        load.wait()
    row = lax.broadcasted_iota(jnp.int32, (rows, template_count), 0)
    column = lax.broadcasted_iota(jnp.int32, (rows, template_count), 1)
    chosen = jnp.full((rows, template_count), -1, jnp.int32)
    for d in range(detections):
        chosen = jnp.where(row == d, kinds[d], chosen)
    onehot[...] = (chosen == column).astype(jnp.float32).astype(jnp.bfloat16)
    mask[...] = jnp.zeros_like(mask)
    mask[:detections, :] = used_raw[...].astype(jnp.float32)

    flat = channels * template_len
    picked = lax.dot_general(onehot[...], normed[...].reshape(flat, template_count), (((1,), (1,)), ((), ())),
                             preferred_element_type=jnp.float32)
    for c in range(channels):
        picks[c] = picked[:, c * template_len:(c + 1) * template_len].astype(jnp.bfloat16)
    last = tm == tm_count - 1

    @pl.when(jnp.logical_not(last))
    def _():
        halo_copy.wait_recv()
        ext[:, block_len:block_len + border] = halo[:, :border].astype(jnp.float32)

    @pl.when(last)
    def _():
        ext[:, block_len:block_len + border] = tail[...].astype(jnp.float32)

    @pl.when(tm > 0)
    def _():
        halo_copy.wait_send()

    ext[:, :block_len] = record[...].astype(jnp.float32)
    lane = lax.broadcasted_iota(jnp.int32, (channels, width), 1)
    sums = jnp.where(lane < block_len + border, ext[...], 0.0)
    squares = sums * sums

    def left(x, by):
        return pltpu.roll(x, width - by, 1)

    def window_sum(x):
        out, offset, span = None, 0, 1
        powers = []
        while span <= template_len:
            powers.append((span, x))
            if span * 2 <= template_len:
                x = x + left(x, span)
            span *= 2
        for span, value in reversed(powers):
            if template_len & span:
                value = value if offset == 0 else left(value, offset)
                out = value if out is None else out + value
                offset += span
        return out[:, :windows]

    for r in range(8):
        moved = sums if r == 0 else left(sums, r)
        for j in range(width // 128):
            shifts[j, pl.ds(r, channels, stride=8), :] = moved[:, j * 128:j * 128 + 128]
    average = window_sum(sums) * (1.0 / template_len)
    square = window_sum(squares) * (1.0 / template_len)
    row = lax.broadcasted_iota(jnp.int32, (channels, windows), 0)
    alive = jnp.zeros((channels, windows), jnp.float32)
    for c in range(channels):
        alive = jnp.where(row == c, live[c].astype(jnp.float32), alive)
    mean[...] = average
    weight[...] = alive / jnp.sqrt(template_len * (square - average * average + EPSILON))

    def unfold(step, carry):
        for g in range(PAIR):
            c = step * PAIR + g
            trace = jnp.concatenate(
                [shifts[j, pl.ds(pl.multiple_of(c * 8, 8), 8), :] for j in range(width // 128)], axis=1)
            weights = weight[pl.ds(c, 1), :block_len]
            average = mean[pl.ds(c, 1), :block_len]
            raw, fine = {}, {}
            for s in range(0, 16, 2):
                upper = trace if s == 0 else pltpu.roll(trace, width - 8 * s, 1)
                both = jnp.concatenate([upper, pltpu.roll(trace, width - 8 * s - 8, 1)], axis=0)
                for low in range(0, template_len, 128):
                    first = low + 8 * s
                    used = min(16, template_len - first)
                    if used > 0:
                        piece = both[:used, low:low + windows]
                        raw[first] = piece.astype(jnp.bfloat16)
                        fine[first] = ((piece[:, :block_len] - average) * weights).astype(jnp.bfloat16)
            order = sorted(raw)
            unfolded[c] = jnp.concatenate([raw[k] for k in order], axis=0)
            scaled[c] = jnp.concatenate([fine[k] for k in order], axis=0)
        return carry

    lax.fori_loop(0, channels // PAIR, unfold, 0)

    count = block.shape[0]
    blocks = template_count // count
    each = count // (2 * own_rows)

    def to_sibling(q):
        return pltpu.make_async_remote_copy(
            src_ref=sibling_out.at[q], dst_ref=sibling_in.at[q],
            send_sem=ss_sem.at[q], recv_sem=sr_sem.at[q],
            device_id=(tm, sibling), device_id_type=MESH)

    def to_chip(off):
        return pltpu.make_async_remote_copy(
            src_ref=pair_out.at[off], dst_ref=landed.at[off],
            send_sem=ps_sem.at[off], recv_sem=pr_sem.at[off],
            device_id=(tm, lax.rem(chip + off, chips) * 2 + core), device_id_type=MESH)

    def pass_on(b):
        for j in range(each):
            q = b * each + j
            to_sibling(q).wait_recv()
            off = lax.rem(q - chip + chips, chips)

            @pl.when(off > 0)
            def _():
                pair_out[off] = (kept[q] + sibling_in[q].astype(jnp.float32)).astype(jnp.bfloat16)
                to_chip(off).start()

    home = chip // each

    def nth(i):
        flip, out, bit = blocks - 1 - i, 0, 1
        while bit < blocks:
            digit = lax.rem(home // bit, 2)
            out = out + bit * (1 - digit if flip & bit else digit)
            bit *= 2
        return out

    for i in range(blocks):
        b = nth(i)
        if i == 1:
            span = lag_count + 128
            values[...] = jnp.zeros_like(values)

            def find(step, carry):
                for g in range(4):
                    c = step * 4 + g
                    found = jnp.dot(picks[c], unfolded[c], preferred_element_type=jnp.float32)
                    lane = lax.broadcasted_iota(jnp.int32, mask.shape, 1)
                    used = jnp.sum(jnp.where(lane == c, mask[...], 0.0), axis=1, keepdims=True)
                    found = found * weight[pl.ds(c, 1), :] * used
                    for j in range(windows // 128):
                        series[j, pl.ds(pl.multiple_of(c * rows, rows), rows), :] = found[:, j * 128:j * 128 + 128]
                return carry

            lax.fori_loop(0, channels // 4, find, 0)
            pass_on(nth(i - 1))

            def cut(d):
                start = jnp.clip(starts[d] - tm * block_len, 0, block_len - 1)
                base = lax.shift_right_logical(start, 7)
                piece = jnp.concatenate(
                    [series[base + j, pl.ds(d, channels, stride=rows), :] for j in range(span // 128)], axis=1)
                moved = pltpu.roll(piece, span - (start - base * 128), 1)
                values[pl.ds(pl.multiple_of(d * channels, channels), channels), :] = (
                    moved[:, :lag_count].astype(jnp.bfloat16))

            run = max(n for n in range(1, 9) if detections % n == 0)

            def cut_some(step, carry):
                for g in range(run):
                    cut(step * run + g)
                return carry

            lax.fori_loop(0, detections // run, cut_some, 0)
            columns = values.shape[0]
            earlier = lax.broadcasted_iota(jnp.int32, (rows, columns), 0)
            spot = lax.broadcasted_iota(jnp.int32, (rows, columns), 1)
            now = spot // channels
            by_row = jnp.full((rows, columns), -1, jnp.int32)
            by_column = jnp.full((rows, columns), -2, jnp.int32)
            for d in range(detections):
                by_row = jnp.where(earlier == d, owners[d], by_row)
                by_column = jnp.where(now == d, owners[d], by_column)
            same = jnp.where((by_row == by_column) & (earlier < now), 1.0, 0.0)
            rank = jnp.sum(same, axis=0, keepdims=True).astype(jnp.int32)
            slot = by_column[:1] * CAP + rank
            place = slot * channels + (spot - now * channels)[:1]
            part = CAP * channels
            for off in list(range(1, sta_count)) + [0]:
                peer = lax.rem(me + off, sta_count)
                target = lax.broadcasted_iota(jnp.int32, (part, columns), 0) + peer * part
                putting = (target == place).astype(jnp.float32).astype(jnp.bfloat16)
                filled = jnp.dot(putting, values[...], preferred_element_type=jnp.float32)
                packed[pl.ds(peer * CAP, CAP)] = filled.astype(jnp.bfloat16).reshape(CAP, channels, lag_count)

            mine = xcorr_ref.at[:, pl.ds(pl.multiple_of(me * channels, channels), channels), :]
            sent = []
            for off in range(1, sta_count):
                peer = lax.rem(me + off, sta_count)
                copy = pltpu.make_async_remote_copy(
                    src_ref=packed.at[pl.ds(peer * CAP, CAP)], dst_ref=mine,
                    send_sem=xs_sem.at[off - 1], recv_sem=xr_sem.at[off - 1],
                    device_id=(tm, peer), device_id_type=MESH)
                copy.start()
                sent.append(copy)
            own = pltpu.make_async_copy(packed.at[pl.ds(me * CAP, CAP)], mine, own_sem)
            own.start()

        block[...] = lax.dot_general(
            normed[:, :, pl.ds(pl.multiple_of(b * count, count), count)].reshape(flat, count),
            scaled[...].reshape(flat, block_len), (((0,), (0,)), ((), ())),
            preferred_element_type=jnp.float32)
        for j in range(each):
            q = b * each + j
            low = (2 * j + core) * own_rows
            other = (2 * j + 1 - core) * own_rows
            sibling_out[q] = block[pl.ds(pl.multiple_of(other, 8), own_rows), :].astype(jnp.bfloat16)
            to_sibling(q).start()
            kept[q] = block[pl.ds(pl.multiple_of(low, 8), own_rows), :]
        if i > 1:
            pass_on(nth(i - 1))
    pass_on(nth(blocks - 1))
    result = kept[chip] + sibling_in[chip].astype(jnp.float32)
    for off in range(1, chips):
        to_chip(off).wait()
        result += landed[off].astype(jnp.float32)
    stack_ref[...] = result
    for q in range(chips):
        to_sibling(q).wait_send()
    own.wait()
    for copy in sent:
        copy.wait()


def local(record, tail, templates, live, det_template, det_start, det_owner, det_mask):
    channels, block_len = record.shape
    template_len, template_count = templates.shape[1:]
    border = tail.shape[1]
    lag_count = border - template_len + 2
    sta_count = lax.axis_size("sta")
    tm_count = lax.axis_size("tm")
    detections = det_owner.shape[0]
    rows = round_up(detections, 16)
    windows = block_len + lag_count
    width = round_up(block_len + border + 1, 128)
    own_rows = template_count // sta_count
    chips = sta_count // 2
    count = max(128, 2 * own_rows)
    bf16, f32, i32 = jnp.bfloat16, jnp.float32, jnp.int32
    dma = pltpu.SemaphoreType.DMA
    anywhere = pl.BlockSpec(memory_space=pl.ANY)
    vmem = pl.BlockSpec(memory_space=pltpu.VMEM)
    return pl.pallas_call(
        functools.partial(kernel, lag_count, sta_count, tm_count),
        in_specs=[anywhere] * 8,
        out_specs=[vmem, vmem],
        out_shape=[
            jax.ShapeDtypeStruct((own_rows, block_len), f32),
            jax.ShapeDtypeStruct((CAP, sta_count * channels, lag_count), bf16)],
        scratch_shapes=[
            pltpu.VMEM(record.shape, bf16),
            pltpu.VMEM(tail.shape, bf16),
            pltpu.VMEM(templates.shape, bf16),
            pltpu.SMEM(live.shape, i32),
            pltpu.SMEM(det_template.shape, i32),
            pltpu.SMEM(det_start.shape, i32),
            pltpu.SMEM(det_owner.shape, i32),
            pltpu.VMEM(det_mask.shape, i32),
            pltpu.VMEM((channels, round_up(border, 128)), bf16),
            pltpu.VMEM(templates.shape, bf16),
            pltpu.VMEM((channels, template_len, block_len), bf16),
            pltpu.VMEM((channels, width), f32),
            pltpu.VMEM((width // 128, channels * 8, 128), f32),
            pltpu.VMEM((channels, windows), f32),
            pltpu.VMEM((channels, windows), f32),
            pltpu.VMEM((channels, template_len, windows), bf16),
            pltpu.VMEM((channels, rows, template_len), bf16),
            pltpu.VMEM((windows // 128, channels * rows, 128), f32),
            pltpu.VMEM((rows * channels, lag_count), bf16),
            pltpu.VMEM((rows, template_count), bf16),
            pltpu.VMEM((rows, channels), f32),
            pltpu.VMEM((sta_count * CAP, channels, lag_count), bf16),
            pltpu.VMEM((count, block_len), f32),
            pltpu.VMEM((chips, own_rows, block_len), f32),
            pltpu.VMEM((chips, own_rows, block_len), bf16),
            pltpu.VMEM((chips, own_rows, block_len), bf16),
            pltpu.VMEM((chips, own_rows, block_len), bf16),
            pltpu.VMEM((chips, own_rows, block_len), bf16),
            dma((7,)), dma((CHUNKS,)), dma((2,)),
            dma((sta_count - 1,)), dma((sta_count - 1,)), dma,
            dma((chips,)), dma((chips,)), dma((chips,)), dma((chips,))],
        compiler_params=pltpu.CompilerParams(
            collective_id=0, has_side_effects=True, vmem_limit_bytes=56 * 1024 * 1024),
    )(record, tail, templates, live, det_template, det_start, det_owner, det_mask)


def solution(mesh):
    in_specs = (
        P("sta", "tm"),
        P("sta", None),
        P("sta", None, None),
        P("sta"),
        P("tm"),
        P("tm"),
        P("tm"),
        P("tm", "sta"),
    )
    out_specs = (P("sta", "tm"), P(("tm", "sta"), None, None))
    return jax.shard_map(local, mesh=mesh, in_specs=in_specs, out_specs=out_specs, check_vma=False)
```
